128 devices in a mesh: station: 16 (over x, y), band: 8 (over z, core).
Axes of the slice: x: 4, y: 4, z: 4, core: 2. Of those that a mesh axis runs over, the one named last changes fastest.
Arguments:
- spectra: bfloat16 [2, 512, 32, 8192], P(None, 'band', None, 'station'), may hold values from -6 to 6
- widths: int32 [512], P('band'), may hold values from 1 to 8
- tile_owner: int32 [256, 1], P('station'), may hold values from 0 to 7; in each aligned block of 16 rows (0 to 15, 16 to 31, ...) at most 4 rows name the same one
Outputs:
- delivered: float32 [16, 8, 4, 3, 256, 256], P('station', 'band')
The draws below stay inside these ranges and needn't reach their ends.
Inputs may be any that keep to these rules, and one draw needn't show every extreme that they name: `tile_owner`: within the rows of one station block (aligned blocks of 16 rows) no owner appears more than 4 times.
All inputs are finite; a program needn't handle non-finite values.
Results may differ from the reference program's by a relative error of at most 0.007.
Values may be sent and summed in bfloat16 or wider, within the bound.
No kernel may reach another device: no remote copies, remote signals or barrier semaphores. Data moves between devices by JAX's collectives and lax.ppermute only.
A program may use at most 128 MiB of HBM per device.

```python
import math
import jax
import jax.numpy as jnp
import numpy as np
from jax import lax

TILE = 256
TDEV = 2
BIN_DEV = 64
TW = 32
LAGS = 3
ROUNDS = 4
WMAX = 8
CAP = 4
BINS = 512
CHANNELS = 8192
N_STATION = 16
N_BAND = 8


def touch_ends(entries, own_key, smallest, top_value):
    spot = [jax.random.randint(jax.random.fold_in(own_key, axis), (), 0, length) for axis, length in enumerate(entries.shape)]
    widest = entries.shape.index(max(entries.shape))
    beside = spot[:widest] + [(spot[widest] + 1) % entries.shape[widest]] + spot[widest + 1:]
    return entries.at[tuple(spot)].set(smallest).at[tuple(beside)].set(top_value)


def steps_of(stream_key, shape, split, least, high):
    loudness, own = 1.0, jax.random.fold_in(stream_key, 6)
    for dim, parts in split:
        draws = jnp.exp(jax.random.uniform(jax.random.fold_in(own, dim), (parts,), jnp.float32, least / len(split), high / len(split)))
        loudness = loudness * jnp.repeat(draws, shape[dim] // parts).reshape([-1 if axis == dim else 1 for axis in range(len(shape))])
    return loudness


def routed_block(rng, own, number, rows, amount, top, limit, skew):
    order = jax.random.permutation(rng, amount)
    crowded, common = load_shares(amount, rows * top, limit, skew, True), load_shares(amount, rows * top, limit, skew, False)
    places = jnp.arange(amount)

    def named(lengths, rotation):
        used = int((lengths > 0).sum())
        fixed = max(1, used // 4)
        shifted = fixed + (places - fixed + rotation * (used - fixed)) % max(1, amount - fixed)
        return jnp.zeros((amount,), jnp.int32).at[order[jnp.where(places < fixed, places, shifted)]].set(jnp.asarray(lengths, jnp.int32))

    lengths = jnp.where(number % 4 == 0, named(crowded, number // 4), named(common, number - number // 4 - 1))
    mixed = jax.random.permutation(jax.random.fold_in(own, 3), amount)
    giver, taker = mixed[0:amount // 2 * 2:2], mixed[1:amount // 2 * 2:2]
    slack = jnp.minimum(lengths[giver] - 1, limit - lengths[taker]) // 2
    slack = jnp.where((giver == order[0]) | (taker == order[0]) | (lengths[taker] == 0), 0, jnp.maximum(slack, 0))
    shifted = jax.random.randint(jax.random.fold_in(own, 4), (amount // 2,), 0, 1 << 20) % (slack + 1)
    lengths = lengths.at[giver].add(-shifted).at[taker].add(shifted)
    members = jnp.searchsorted(jnp.cumsum(lengths), jnp.arange(rows * top), side="right").astype(jnp.int32)
    grid = members.reshape(top, rows).T
    grid = grid[jax.random.permutation(jax.random.fold_in(own, 1), rows)]
    rotation = jax.random.randint(jax.random.fold_in(own, 2), (rows, 1), 0, top)
    return jnp.take_along_axis(grid, (jnp.arange(top)[None, :] + rotation) % top, axis=1)


def load_shares(count, total, bound, lean, full):
    loads = [(1 << 20) // math.isqrt(grade ** lean) + 1 for grade in range(1, count + 1)]
    largest = bound if full else min(bound, max(-(-total // count), total * loads[0] // sum(loads)))
    least = 1 if total - largest >= count - 1 else 0
    holding, spare = [largest] + [least] * (count - 1), total - largest - least * (count - 1)
    while spare > 0:
        candidates = [i for i in range(1, count) if holding[i] < largest] or [i for i in range(1, count) if holding[i] < bound]
        whole, left = sum([loads[i] for i in candidates]), spare
        for i in candidates:
            extra = min(bound - holding[i], max(1, left * loads[i] // whole), spare)
            holding[i] = holding[i] + extra
            spare = spare - extra
    return np.array(holding)


def bell_draw(rng, extent, width, limit, pieces=(), dtype=jnp.bfloat16):
    drawn = jax.random.normal(rng, extent, jnp.float32) * width
    if len(pieces) > 0:
        drawn = steps_of(rng, extent, pieces, -0.22, 0.18) * drawn
    return jnp.clip(drawn, min=-limit, max=limit).astype(dtype)


def setup_inputs(seed: int = 0) -> dict:
    arg_keys = jax.random.split(jax.random.key(seed), 4)
    spectra = bell_draw(arg_keys[0], (2, BINS, TW, CHANNELS), 1.0, 6.0, ((1, 8), (3, 16)))
    widths = touch_ends(jax.random.randint(arg_keys[1], (BINS,), 1, WMAX + 1), jax.random.fold_in(arg_keys[1], 1), 1, WMAX).astype(jnp.int32)
    tile_owner_keys = jax.random.split(jax.random.fold_in(arg_keys[2], 1), (N_STATION * ROUNDS * TDEV * TDEV) // (ROUNDS * TDEV * TDEV))
    tile_owner_turns = jax.random.permutation(jax.random.fold_in(arg_keys[2], 3), (N_STATION * ROUNDS * TDEV * TDEV) // (ROUNDS * TDEV * TDEV))
    tile_owner = jax.vmap(lambda own, number: routed_block(jax.random.fold_in(arg_keys[2], 2), own, number, ROUNDS * TDEV * TDEV, N_BAND, 1, CAP, 2))(tile_owner_keys, tile_owner_turns).reshape((N_STATION * ROUNDS * TDEV * TDEV, 1))
    return dict(spectra=spectra, widths=widths, tile_owner=tile_owner)


def reference(spectra, widths, tile_owner):
    width_ch = TDEV * TILE
    tiles_block = ROUNDS * TDEV * TDEV
    wide = spectra.astype(jnp.float32)
    energy = wide[0] * wide[0] + wide[1] * wide[1]
    padded = jnp.pad(energy, ((WMAX, WMAX), (0, 0), (0, 0)))
    bin_index = jnp.arange(BINS)
    summed_energy = jnp.zeros(energy.shape, jnp.float32)
    bin_count = jnp.zeros((BINS,), jnp.float32)
    for offset in range(-WMAX, WMAX + 1):
        inside = (abs(offset) <= widths) & (bin_index + offset >= 0) & (bin_index + offset < BINS)
        weight = jnp.where(inside, 1.0, 0.0).astype(jnp.float32)
        summed_energy = summed_energy + weight[:, None, None] * padded[WMAX + offset:WMAX + offset + BINS]
        bin_count = bin_count + weight
    root_mean = jnp.sqrt(summed_energy / bin_count[:, None, None])
    divisor = 1.0 / jnp.maximum(root_mean, 0.25)
    whitened = (wide * divisor[None]).astype(jnp.bfloat16)
    lag_index = jnp.arange(LAGS).astype(jnp.float32)
    phase_angle = 2.0 * math.pi * (bin_index.astype(jnp.float32)[:, None] * lag_index[None, :]) / BINS
    cosine = jnp.cos(phase_angle).T[:, :, None, None]
    sine_table = jnp.sin(phase_angle).T[:, :, None, None]
    normalize = 1.0 / math.sqrt(BINS * TW)

    def one_block(block):
        start = (block * width_ch).astype(jnp.int32)
        own = lax.dynamic_slice_in_dim(whitened, start, width_ch, 3).astype(jnp.float32)
        turned_re = own[0][None] * cosine + own[1][None] * sine_table
        turned_im = own[1][None] * cosine - own[0][None] * sine_table
        turned = jnp.stack([turned_re, turned_im], axis=1).astype(jnp.bfloat16).astype(jnp.float32)
        turned = turned.reshape(LAGS, 2, N_BAND, BIN_DEV, TW, width_ch)
        rounds_out = []
        for step in range(1, ROUNDS + 1):
            partner_start = ((block - step) % N_STATION * width_ch).astype(jnp.int32)
            partner = lax.dynamic_slice_in_dim(whitened, partner_start, width_ch, 3).astype(jnp.float32)
            partner = partner.reshape(2, N_BAND, BIN_DEV, TW, width_ch)
            grouped = jnp.einsum('lrgftc,rgftd->glcd', turned, partner, precision=lax.Precision.HIGHEST)
            grouped = (grouped * normalize).astype(jnp.bfloat16).astype(jnp.float32)
            rounds_out.append(lax.optimization_barrier(jnp.sum(grouped, axis=0)))
        values = jnp.stack(rounds_out)
        values = values.reshape(ROUNDS, LAGS, TDEV, TILE, TDEV, TILE).transpose(0, 2, 4, 1, 3, 5)
        values = values.reshape(tiles_block, LAGS * TILE * TILE)
        owners = lax.dynamic_slice_in_dim(tile_owner[:, 0], (block * tiles_block).astype(jnp.int32), tiles_block, 0)
        order = jnp.arange(tiles_block)
        earlier = (order[:, None] > order[None, :]) & (owners[:, None] == owners[None, :])
        slot_index = lax.optimization_barrier(jnp.sum(jnp.where(earlier, 1, 0), axis=1)).astype(jnp.int32)
        rows = jnp.arange(N_BAND * CAP)
        placing = (owners[None, :] == (rows // CAP)[:, None]) & (slot_index[None, :] == (rows % CAP)[:, None])
        placing = jnp.where(placing, 1.0, 0.0).astype(jnp.float32)
        result = jnp.dot(placing, values, precision=lax.Precision.HIGHEST, preferred_element_type=jnp.float32)
        return result.reshape(N_BAND, CAP, LAGS, TILE, TILE)
    return lax.map(one_block, jnp.arange(N_STATION).astype(jnp.int32))
```

```python
import math

import jax
import jax.numpy as jnp
from jax import lax
from jax.sharding import PartitionSpec as P

TILE = 256
TDEV = 2
LAGS = 3
ROUNDS = 4
WMAX = 8
CAP = 4


def with_halo(block, width):
    count = lax.axis_size("band")
    forward = [(i, i + 1) for i in range(count - 1)]
    backward = [(target, source) for source, target in forward]
    low = lax.ppermute(block[:, block.shape[1] - width :], "band", forward)
    high = lax.ppermute(block[:, :width], "band", backward)
    return jnp.concatenate([low, block, high], axis=1)


def along_station(value, dx, dy):
    pairs = []
    for x in range(4):
        for y in range(4):
            pairs.append((4 * x + y, 4 * ((x + dx) % 4) + (y + dy) % 4))
    return lax.ppermute(value, "station", pairs)


def along_band(value, target):
    return lax.ppermute(value, "band", [(i, target(i)) for i in range(8)])


def swap_core(value):
    return along_band(value, lambda g: g ^ 1)


def swap_near(value):
    return along_band(value, lambda g: g ^ 2)


def swap_far(value):
    return along_band(value, lambda g: 2 * (3 - g // 2) + g % 2)


def whiten(spectra, widths, first_bin, bins_all):
    bin_dev, windows, width_ch = spectra.shape[1:]
    padded = with_halo(spectra, WMAX)
    wide = padded.astype(jnp.float32)
    energy = wide[0] * wide[0] + wide[1] * wide[1]
    local_bins = first_bin + jnp.arange(bin_dev)
    summed_energy = jnp.zeros((bin_dev, windows, width_ch), jnp.float32)
    bin_count = jnp.zeros((bin_dev,), jnp.float32)
    for offset in range(-WMAX, WMAX + 1):
        inside = (
            (abs(offset) <= widths) & (local_bins + offset >= 0) & (local_bins + offset < bins_all)
        )
        weight = jnp.where(inside, 1.0, 0.0).astype(jnp.float32)
        summed_energy = (
            summed_energy + weight[:, None, None] * energy[WMAX + offset : WMAX + offset + bin_dev]
        )
        bin_count = bin_count + weight
    root_mean = jnp.sqrt(summed_energy / bin_count[:, None, None])
    divisor = 1.0 / jnp.maximum(root_mean, 0.25)
    return (spectra.astype(jnp.float32) * divisor[None]).astype(jnp.bfloat16)


def turn(block, angle, sign):
    cosine = jnp.cos(angle).T[:, :, None, None]
    sine = sign * jnp.sin(angle).T[:, :, None, None]
    real = block[0].astype(jnp.float32)[None]
    imag = block[1].astype(jnp.float32)[None]
    return jnp.stack([real * cosine + imag * sine, imag * cosine - real * sine], axis=1).astype(
        jnp.bfloat16
    )


def correlate(first, second, normalize):
    if first.ndim == 5:
        product = lax.dot_general(
            first, second, (((1, 2, 3), (0, 1, 2)), ((), ())), preferred_element_type=jnp.float32
        )
    else:
        product = lax.dot_general(
            first, second, (((0, 1, 2), (1, 2, 3)), ((), ())), preferred_element_type=jnp.float32
        ).transpose(1, 0, 2)
    return (product * normalize).astype(jnp.bfloat16)


def plus(a, b):
    return a.astype(jnp.float32) + b.astype(jnp.float32)


def pick(value, axis, index):
    return lax.dynamic_index_in_dim(value, index, axis, keepdims=False)


def reduce_band(pair, core, near, far):
    split = pair.reshape(2, LAGS, TDEV, 2, 4, 32, TDEV * TILE)
    got = swap_core(pick(split, 3, 1 - core))
    both = plus(pick(split, 3, core), got).astype(jnp.bfloat16)
    both = both.reshape(2, LAGS, TDEV, 2, 2, 32, TDEV * TILE)
    a, b = both[0], both[1]
    got_a = swap_near(pick(a, 2, 1 - near))
    got_b = swap_far(pick(b, 3, 1 - far))
    a = plus(pick(a, 2, near), got_a).astype(jnp.bfloat16)
    b = plus(pick(b, 3, far), got_b).astype(jnp.bfloat16)
    got_a = swap_far(pick(a, 2, 1 - far))
    got_b = swap_near(pick(b, 2, 1 - near))
    a = plus(pick(a, 2, far), got_a).astype(jnp.bfloat16)
    b = plus(pick(b, 2, near), got_b).astype(jnp.bfloat16)
    return a, b


def body(spectra, widths, tile_owner):
    bin_dev = spectra.shape[1]
    windows = spectra.shape[2]
    half = bin_dev // 2
    band = lax.axis_index("band")
    station = lax.axis_index("station")
    row = station % 4
    depth, core = band // 2, band % 2
    far = depth // 2
    near = (depth % 2) ^ far
    bins_all = bin_dev * lax.axis_size("band")
    first_bin = band * bin_dev
    whitened = whiten(spectra, widths, first_bin, bins_all)
    up, down = whitened[:, :half], whitened[:, half:]

    send_next = jnp.where(row < 3, up, down)
    send_back = jnp.where(row > 0, down, up)
    send_two = jnp.where(row < 2, up, down)
    from_left = along_station(up, 1, 0)
    from_right = along_station(down, -1, 0)
    blocks = [
        (along_station(send_next, 0, 1), row >= 1),
        (along_station(send_back, 0, -1), row == 3),
        (along_station(send_two, 0, 2), row >= 2),
    ]

    lag_index = jnp.arange(LAGS).astype(jnp.float32)
    local_bins = (first_bin + jnp.arange(bin_dev)).astype(jnp.float32)
    angle = 2.0 * math.pi * (local_bins[:, None] * lag_index[None, :]) / bins_all
    angle_up, angle_down = angle[:half], angle[half:]
    normalize = 1.0 / math.sqrt(bins_all * windows)

    pairs = [
        jnp.stack(
            [
                correlate(up, turn(from_left, angle_up, -1.0), normalize),
                correlate(from_right, turn(down, angle_down, -1.0), normalize),
            ]
        )
    ]
    for block, lower in blocks:
        angle_here = jnp.where(lower, angle_up, angle_down)
        first = turn(jnp.where(lower, up, from_right), angle_here, 1.0)
        second = turn(jnp.where(lower, from_left, down), angle_here, -1.0)
        pairs.append(
            jnp.stack(
                [correlate(first, block, normalize), correlate(block, second, normalize)]
            )
        )
    reduced = [reduce_band(pair, core, near, far) for pair in pairs]
    (same_a, same_b), (next_a, next_b), (back_a, back_b), (two_a, two_b) = reduced
    same_b = along_station(same_b, 1, 0)
    next_a = jnp.where(row >= 1, next_a, along_station(next_a, 1, 0))
    back_a = jnp.where(row == 3, back_a, along_station(back_a, 1, 0))
    two_a = jnp.where(row >= 2, two_a, along_station(two_a, 1, 0))
    next_b = along_station(next_b, 0, -1)
    back_b = along_station(back_b, 0, 1)
    two_b = along_station(two_b, 0, 2)
    value = jnp.stack(
        [plus(next_a, back_b), plus(two_a, two_b), plus(back_a, next_b), plus(same_a, same_b)]
    ).astype(jnp.bfloat16)
    value = value.reshape(ROUNDS, LAGS, TDEV, 32, TDEV, TILE).transpose(0, 2, 4, 1, 3, 5)
    tiles_block = tile_owner.shape[0]
    value = value.reshape(tiles_block, LAGS * 32 * TILE)

    owners = tile_owner[:, 0]
    order = jnp.arange(tiles_block)
    earlier = (order[:, None] > order[None, :]) & (owners[:, None] == owners[None, :])
    slot_index = jnp.sum(jnp.where(earlier, 1, 0), axis=1).astype(jnp.int32)
    rows = jnp.arange(8 * CAP)
    placing = (owners[None, :] == (rows // CAP)[:, None]) & (
        slot_index[None, :] == (rows % CAP)[:, None]
    )
    placing = jnp.where(placing, 1.0, 0.0).astype(jnp.bfloat16)
    buffer = jnp.dot(placing, value, preferred_element_type=jnp.float32).astype(jnp.bfloat16)
    buffer = buffer.reshape(8, CAP, LAGS, 32, TILE)
    arrived = lax.all_to_all(buffer, "band", split_axis=0, concat_axis=0, tiled=True)
    pieces = [arrived[2 * z + c] for c in range(2) for z in (0, 3, 1, 2)]
    result = jnp.stack(pieces, axis=2).astype(jnp.float32)
    return result.reshape(1, 1, CAP, LAGS, TILE, TILE)


def solution(mesh):
    return jax.shard_map(
        body,
        mesh=mesh,
        in_specs=(P(None, "band", None, "station"), P("band"), P("station", None)),
        out_specs=P("station", "band", None, None, None, None),
        check_vma=False,
    )
```

```python
import functools
import math

import jax
import jax.numpy as jnp
from jax import lax
from jax.experimental import pallas as pl
from jax.experimental.pallas import tpu as pltpu
from jax.sharding import PartitionSpec as P

TILE = 256
TDEV = 2
LAGS = 3
ROUNDS = 4
WMAX = 8
CAP = 4
CH = TILE * TDEV
WIN = 32


def edge_kernel(normalize, choose, half, info, tab, *refs):
    if choose:
        f_hbm, t_up, t_down, q_up, q_down, mine, other, f_buf, t_buf, q_buf, ft, tt, qt, sems = refs
    else:
        fa_hbm, fb_hbm, t_hbm, q_hbm, mine, other, f_buf, fb_buf, t_buf, q_buf, ft, ftb, tt, qt, sems = refs
    lag = pl.program_id(0)
    core = info[1]
    rows = 2 * half * WIN

    def turn(buf, out, which, k):
        for b in range(half):
            span = pl.ds(b * WIN, WIN)
            re, im = buf[0, b].astype(jnp.float32), buf[1, b].astype(jnp.float32)
            c, s = tab[which, 0, k, b], tab[which, 1, k, b]
            out[0, span] = (re * c + im * s).astype(jnp.bfloat16)
            out[1, span] = (im * c - re * s).astype(jnp.bfloat16)

    def transpose(buf, out):
        flat = buf[...].reshape(rows, CH)
        for h in range(rows // 512):
            out[:, h * 512 : (h + 1) * 512] = flat[h * 512 : (h + 1) * 512].T

    def products(t, q):
        pa = jnp.dot(ft[...], t.reshape(rows, CH), preferred_element_type=jnp.float32).T
        pb = jnp.dot((ft if choose else ftb)[...], q.reshape(rows, CH), preferred_element_type=jnp.float32)
        for e, p in ((0, pa), (1, pb)):
            p = (p * normalize).astype(jnp.bfloat16)
            for i in range(2):
                lo, hi = p[i * 256 : i * 256 + 128], p[i * 256 + 128 : i * 256 + 256]
                mine[e, 0, i] = jnp.where(core == 0, lo, hi)
                other[e, 0, i] = jnp.where(core == 0, hi, lo)

    @pl.when(lag == 0)
    def _():
        if choose:
            pltpu.make_async_copy(f_hbm, f_buf, sems.at[0]).start()
            lower = info[0] > 0

            @pl.when(lower)
            def _():
                pltpu.make_async_copy(t_up, t_buf, sems.at[1]).start()
                pltpu.make_async_copy(q_up, q_buf, sems.at[2]).start()

            @pl.when(jnp.logical_not(lower))
            def _():
                pltpu.make_async_copy(t_down, t_buf, sems.at[1]).start()
                pltpu.make_async_copy(q_down, q_buf, sems.at[2]).start()

            pltpu.make_async_copy(f_hbm, f_buf, sems.at[0]).wait()
            transpose(f_buf, ft)
            pltpu.make_async_copy(t_up, t_buf, sems.at[1]).wait()
            pltpu.make_async_copy(q_up, q_buf, sems.at[2]).wait()
        else:
            copies = [
                pltpu.make_async_copy(src, dst, sems.at[n])
                for n, (src, dst) in enumerate(
                    ((fa_hbm, f_buf), (fb_hbm, fb_buf), (t_hbm, t_buf), (q_hbm, q_buf))
                )
            ]
            for copy in copies:
                copy.start()
            copies[0].wait()
            transpose(f_buf, ft)
            copies[1].wait()
            transpose(fb_buf, ftb)
            copies[2].wait()
            copies[3].wait()

    @pl.when(lag == 0)
    def _():
        turn(t_buf, tt, 0, 0)
        turn(q_buf, qt, 1, 0)
        products(t_buf[...], q_buf[...])

    @pl.when(lag == 1)
    def _():
        products(tt[...], qt[...])

    @pl.when(lag == 2)
    def _():
        turn(t_buf, tt, 0, 1)
        turn(q_buf, qt, 1, 1)
        products(tt[...], qt[...])


def edges(info, tab, blocks, normalize):
    half = blocks[0].shape[1]
    choose = len(blocks) == 5
    shape = (2, LAGS, 2, 128, CH)
    part = (2, 1, 2, 128, CH)
    buf = pltpu.VMEM((2, half, WIN, CH), jnp.bfloat16)
    flipped = pltpu.VMEM((CH, 2 * half * WIN), jnp.bfloat16)
    turned = pltpu.VMEM((2, half * WIN, CH), jnp.bfloat16)
    if choose:
        scratch = [buf] * 3 + [flipped] + [turned] * 2 + [pltpu.SemaphoreType.DMA((3,))]
    else:
        scratch = [buf] * 4 + [flipped] * 2 + [turned] * 2 + [pltpu.SemaphoreType.DMA((4,))]
    return pl.pallas_call(
        functools.partial(edge_kernel, normalize, choose, half),
        grid_spec=pltpu.PrefetchScalarGridSpec(
            num_scalar_prefetch=2,
            grid=(LAGS,),
            in_specs=[pl.BlockSpec(memory_space=pl.ANY)] * len(blocks),
            out_specs=[pl.BlockSpec(part, lambda l, info, tab: (0, l, 0, 0, 0))] * 2,
            scratch_shapes=scratch,
        ),
        out_shape=[jax.ShapeDtypeStruct(shape, jnp.bfloat16)] * 2,
        compiler_params=pltpu.CompilerParams(vmem_limit_bytes=40 * 1024 * 1024),
        cost_estimate=pl.CostEstimate(
            flops=2 * 2 * LAGS * CH * CH * half * 2 * WIN, bytes_accessed=10 * 2**20, transcendentals=0
        ),
    )(info, tab, *blocks)


def whiten_kernel(bin_dev, info, widths, inverse, low, mid, high, up, down, to_next, to_back, to_two, run):
    row = info[0]
    half = bin_dev // 2

    def energy(ref, at):
        re, im = ref[0, at].astype(jnp.float32), ref[1, at].astype(jnp.float32)
        return re * re + im * im

    total = jnp.zeros(run.shape[1:], jnp.float32)
    run[0] = total
    for i in range(WMAX):
        total = total + energy(low, i)
        run[i + 1] = total
    for i in range(bin_dev):
        total = total + energy(mid, i)
        run[i + WMAX + 1] = total
    for i in range(WMAX):
        total = total + energy(high, i)
        run[WMAX + bin_dev + i + 1] = total

    def whitened(f):
        w = widths[f]
        mean = (run[f + WMAX + 1 + w] - run[f + WMAX - w]) * inverse[f]
        scale = lax.rsqrt(jnp.maximum(mean, 0.0625))
        return [(mid[part, f].astype(jnp.float32) * scale).astype(jnp.bfloat16) for part in range(2)]

    for f in range(half):
        u = whitened(f)
        d = whitened(f + half)
        for part in range(2):
            up[part, f] = u[part]
            down[part, f] = d[part]
            to_next[part, f] = jnp.where(row < 3, u[part], d[part])
            to_back[part, f] = jnp.where(row > 0, d[part], u[part])
            to_two[part, f] = jnp.where(row < 2, u[part], d[part])


def whiten(info, widths, inverse, low, mid, high, rows=16, lanes=256):
    bin_dev = mid.shape[1]
    grid = (WIN // rows, CH // lanes)

    def spec(bins):
        return pl.BlockSpec((2, bins, rows, lanes), lambda w, c, *_: (0, 0, w, c))

    out = jax.ShapeDtypeStruct((2, bin_dev // 2, WIN, CH), jnp.bfloat16)
    return pl.pallas_call(
        functools.partial(whiten_kernel, bin_dev),
        grid_spec=pltpu.PrefetchScalarGridSpec(
            num_scalar_prefetch=3,
            grid=grid,
            in_specs=[spec(WMAX), spec(bin_dev), spec(WMAX)],
            out_specs=[spec(bin_dev // 2)] * 5,
            scratch_shapes=[pltpu.VMEM((bin_dev + 2 * WMAX + 1, rows, lanes), jnp.float32)],
        ),
        out_shape=[out] * 5,
        compiler_params=pltpu.CompilerParams(vmem_limit_bytes=40 * 1024 * 1024),
        cost_estimate=pl.CostEstimate(flops=40 * 2**20, bytes_accessed=15 * 2**20, transcendentals=2**20),
    )(info, widths, inverse, low, mid, high)


def along_station(value, dx, dy):
    pairs = []
    for x in range(4):
        for y in range(4):
            pairs.append((4 * x + y, 4 * ((x + dx) % 4) + (y + dy) % 4))
    return lax.ppermute(value, "station", pairs)


def along_band(value, target):
    return lax.ppermute(value, "band", [(i, target(i)) for i in range(8)])


def swap_core(value):
    return along_band(value, lambda g: g ^ 1)


def swap_near(value):
    return along_band(value, lambda g: g ^ 2)


def swap_far(value):
    return along_band(value, lambda g: 2 * (3 - g // 2) + g % 2)


def halo(block):
    forward = [(i, i + 1) for i in range(7)]
    backward = [(target, source) for source, target in forward]
    low = lax.ppermute(block[:, block.shape[1] - WMAX :], "band", forward)
    high = lax.ppermute(block[:, :WMAX], "band", backward)
    return low, high


def plus(a, b):
    return a.astype(jnp.float32) + b.astype(jnp.float32)


def pick(value, axis, index):
    return lax.dynamic_index_in_dim(value, index, axis, keepdims=False)


def reduce_band(mine, other, near, far):
    got = swap_core(other)
    both = plus(mine, got).astype(jnp.bfloat16)
    both = both.reshape(2, LAGS, TDEV, 2, 2, 32, CH)
    a, b = both[0], both[1]
    got_a = swap_near(pick(a, 2, 1 - near))
    got_b = swap_far(pick(b, 3, 1 - far))
    a = plus(pick(a, 2, near), got_a).astype(jnp.bfloat16)
    b = plus(pick(b, 3, far), got_b).astype(jnp.bfloat16)
    got_a = swap_far(pick(a, 2, 1 - far))
    got_b = swap_near(pick(b, 2, 1 - near))
    a = plus(pick(a, 2, far), got_a).astype(jnp.bfloat16)
    b = plus(pick(b, 2, near), got_b).astype(jnp.bfloat16)
    return a, b


def body(spectra, widths, tile_owner):
    bin_dev = spectra.shape[1]
    half = bin_dev // 2
    band = lax.axis_index("band")
    row = lax.axis_index("station") % 4
    depth, core = band // 2, band % 2
    far = depth // 2
    near = (depth % 2) ^ far
    bins_all = bin_dev * 8
    first_bin = band * bin_dev
    normalize = 1.0 / math.sqrt(bins_all * WIN)

    low, high = halo(spectra)
    local_bins = first_bin + jnp.arange(bin_dev)
    count = jnp.minimum(local_bins + widths, bins_all - 1) - jnp.maximum(local_bins - widths, 0) + 1
    inverse = 1.0 / count.astype(jnp.float32)
    row_info = jnp.reshape(row, (1,)).astype(jnp.int32)
    up, down, to_next, to_back, to_two = whiten(
        row_info, widths, inverse, low, spectra, high
    )
    from_left = along_station(up, 1, 0)
    from_right = along_station(down, -1, 0)
    from_next = along_station(to_next, 0, 1)
    from_back = along_station(to_back, 0, -1)
    to_two, from_next, from_back = lax.optimization_barrier((to_two, from_next, from_back))
    from_two = along_station(to_two, 0, 2)

    lag_index = jnp.arange(1, LAGS).astype(jnp.float32)
    angle = 2.0 * math.pi * (local_bins.astype(jnp.float32)[None, :] * lag_index[:, None]) / bins_all
    cosine, sine = jnp.cos(angle), jnp.sin(angle)
    forth = jnp.stack([cosine, sine])
    back = jnp.stack([cosine, -sine])
    forth_up, forth_down = forth[..., :half], forth[..., half:]
    back_up, back_down = back[..., :half], back[..., half:]

    def info_of(lower):
        return jnp.stack([lower.astype(jnp.int32), core.astype(jnp.int32)])

    def table_of(lower):
        return jnp.where(
            lower, jnp.stack([forth_up, back_up]), jnp.stack([forth_down, back_down])
        )

    same = edges(
        info_of(core), jnp.stack([forth_up, back_down]), (from_left, from_right, up, down), normalize
    )
    groups = [same]
    for block, lower in ((from_next, row >= 1), (from_back, row == 3), (from_two, row >= 2)):
        groups.append(
            edges(
                info_of(lower), table_of(lower), (block, up, from_right, from_left, down), normalize
            )
        )
    reduced = [reduce_band(mine, other, near, far) for mine, other in groups]
    (same_a, same_b), (next_a, next_b), (back_a, back_b), (two_a, two_b) = reduced
    same_b = along_station(same_b, 1, 0)
    next_a = jnp.where(row >= 1, next_a, along_station(next_a, 1, 0))
    back_a = jnp.where(row == 3, back_a, along_station(back_a, 1, 0))
    two_a = jnp.where(row >= 2, two_a, along_station(two_a, 1, 0))
    next_b = along_station(next_b, 0, -1)
    back_b = along_station(back_b, 0, 1)
    two_b = along_station(two_b, 0, 2)
    value = jnp.stack(
        [plus(next_a, back_b), plus(two_a, two_b), plus(back_a, next_b), plus(same_a, same_b)]
    ).astype(jnp.bfloat16)
    value = value.reshape(ROUNDS, LAGS, TDEV, 32, TDEV, TILE).transpose(0, 2, 4, 1, 3, 5)
    tiles_block = tile_owner.shape[0]
    value = value.reshape(tiles_block, LAGS * 32 * TILE)

    owners = tile_owner[:, 0]
    order = jnp.arange(tiles_block)
    earlier = (order[:, None] > order[None, :]) & (owners[:, None] == owners[None, :])
    slot_index = jnp.sum(jnp.where(earlier, 1, 0), axis=1).astype(jnp.int32)
    rows = jnp.arange(8 * CAP)
    placing = (owners[None, :] == (rows // CAP)[:, None]) & (
        slot_index[None, :] == (rows % CAP)[:, None]
    )
    placing = jnp.where(placing, 1.0, 0.0).astype(jnp.bfloat16)
    buffer = jnp.dot(placing, value, preferred_element_type=jnp.float32).astype(jnp.bfloat16)
    buffer = buffer.reshape(8, CAP, LAGS, 32, TILE)
    arrived = lax.all_to_all(buffer, "band", split_axis=0, concat_axis=0, tiled=True)
    pieces = [arrived[2 * z + c] for c in range(2) for z in (0, 3, 1, 2)]
    result = jnp.stack(pieces, axis=2).astype(jnp.float32)
    return result.reshape(1, 1, CAP, LAGS, TILE, TILE)


def solution(mesh):
    return jax.shard_map(
        body,
        mesh=mesh,
        in_specs=(P(None, "band", None, "station"), P("band"), P("station", None)),
        out_specs=P("station", "band", None, None, None, None),
        check_vma=False,
    )
```

```python
import functools
import math

import jax
import jax.numpy as jnp
from jax import lax
from jax.experimental import pallas as pl
from jax.experimental.pallas import tpu as pltpu
from jax.sharding import PartitionSpec as P

TILE = 256
TDEV = 2
LAGS = 3
ROUNDS = 4
WMAX = 8
CAP = 4
CH = TILE * TDEV
WIN = 32
CHUNKS = (0, 9, 19, 28, 32)
ROWS_OF = (0, 4, 2, 6, 3, 7, 1, 5)


def edge_kernel(normalize, choose, half, starts, halves, info, tab, *refs):
    pieces = len(starts)
    f_hbm, refs = refs[:pieces], refs[pieces:]
    if choose:
        t_up, t_down, q_up, q_down, *outs, f_buf, t_buf, q_buf, ft, tt, qt, sems = refs
    else:
        fb_hbm, t_hbm, q_hbm, *outs, f_buf, fb_buf, t_buf, q_buf, ft, ftb, tt, qt, sems = refs
    lag = pl.program_id(0)
    core = info[1]
    rows = 2 * half * WIN

    def turn(buf, out, which, k):
        for b in range(half):
            span = pl.ds(b * WIN, WIN)
            re, im = buf[0, b].astype(jnp.float32), buf[1, b].astype(jnp.float32)
            c, s = tab[which, 0, k, b], tab[which, 1, k, b]
            out[0, span] = (re * c + im * s).astype(jnp.bfloat16)
            out[1, span] = (im * c - re * s).astype(jnp.bfloat16)

    def transpose(buf, out):
        flat = buf[...].reshape(rows, CH)
        for h in range(rows // 512):
            out[:, h * 512 : (h + 1) * 512] = flat[h * 512 : (h + 1) * 512].T

    def store(e, p):
        p = (p * normalize).astype(jnp.bfloat16)
        for i in range(2):
            tile = p[i * TILE : (i + 1) * TILE]
            if halves:
                lo, hi = tile[: TILE // 2], tile[TILE // 2 :]
                outs[0][e, 0, i] = jnp.where(core == 0, lo, hi)
                outs[1][e, 0, i] = jnp.where(core == 0, hi, lo)
            else:
                for g in range(8):
                    outs[0][g, e, 0, i] = tile[ROWS_OF[g] * 32 : (ROWS_OF[g] + 1) * 32]

    def product_a(t):
        store(0, jnp.dot(ft[...], t.reshape(rows, CH), preferred_element_type=jnp.float32).T)

    def product_b(q):
        flip = ft if choose else ftb
        store(1, jnp.dot(flip[...], q.reshape(rows, CH), preferred_element_type=jnp.float32))

    @pl.when(lag == 0)
    def _():
        if choose:
            loads = [
                pltpu.make_async_copy(src, f_buf.at[:, pl.ds(starts[n], src.shape[1])], sems.at[2 + n])
                for n, src in enumerate(f_hbm)
            ]
            for load in loads:
                load.start()
            lower = info[0] > 0

            @pl.when(lower)
            def _():
                pltpu.make_async_copy(t_up, t_buf, sems.at[0]).start()
                pltpu.make_async_copy(q_up, q_buf, sems.at[1]).start()

            @pl.when(jnp.logical_not(lower))
            def _():
                pltpu.make_async_copy(t_down, t_buf, sems.at[0]).start()
                pltpu.make_async_copy(q_down, q_buf, sems.at[1]).start()

            for load in loads:
                load.wait()
            transpose(f_buf, ft)
            pltpu.make_async_copy(t_up, t_buf, sems.at[0]).wait()
            pltpu.make_async_copy(q_up, q_buf, sems.at[1]).wait()
        else:
            copies = [
                pltpu.make_async_copy(src, dst, sems.at[n])
                for n, (src, dst) in enumerate(
                    ((f_hbm[0], f_buf), (fb_hbm, fb_buf), (t_hbm, t_buf), (q_hbm, q_buf))
                )
            ]
            for copy in copies:
                copy.start()
            copies[0].wait()
            transpose(f_buf, ft)
            copies[1].wait()
            transpose(fb_buf, ftb)
            copies[2].wait()
            copies[3].wait()
        turn(t_buf, tt, 0, 0)
        turn(q_buf, qt, 1, 0)
        product_a(t_buf[...])
        product_b(q_buf[...])

    @pl.when(lag == 1)
    def _():
        product_a(tt[...])
        product_b(qt[...])

    @pl.when(lag == 2)
    def _():
        turn(t_buf, tt, 0, 1)
        turn(q_buf, qt, 1, 1)
        product_a(tt[...])
        product_b(qt[...])


def edges(info, tab, f_blocks, others, normalize, halves):
    half = others[0].shape[1]
    choose = len(others) == 4
    starts = [sum(block.shape[1] for block in f_blocks[:n]) for n in range(len(f_blocks))]
    if halves:
        shape, part = (2, LAGS, 2, TILE // 2, CH), (2, 1, 2, TILE // 2, CH)
        out_spec = [pl.BlockSpec(part, lambda l, info, tab: (0, l, 0, 0, 0))] * 2
        out_shape = [jax.ShapeDtypeStruct(shape, jnp.bfloat16)] * 2
    else:
        shape, part = (8, 2, LAGS, 2, 32, CH), (8, 2, 1, 2, 32, CH)
        out_spec = pl.BlockSpec(part, lambda l, info, tab: (0, 0, l, 0, 0, 0))
        out_shape = jax.ShapeDtypeStruct(shape, jnp.bfloat16)
    buf = pltpu.VMEM((2, half, WIN, CH), jnp.bfloat16)
    flipped = pltpu.VMEM((CH, 2 * half * WIN), jnp.bfloat16)
    turned = pltpu.VMEM((2, half * WIN, CH), jnp.bfloat16)
    if choose:
        scratch = [buf] * 3 + [flipped] + [turned] * 2
    else:
        scratch = [buf] * 4 + [flipped] * 2 + [turned] * 2
    blocks = (*f_blocks, *others)
    return pl.pallas_call(
        functools.partial(edge_kernel, normalize, choose, half, starts, halves),
        grid_spec=pltpu.PrefetchScalarGridSpec(
            num_scalar_prefetch=2,
            grid=(LAGS,),
            in_specs=[pl.BlockSpec(memory_space=pl.ANY)] * len(blocks),
            out_specs=out_spec,
            scratch_shapes=scratch + [pltpu.SemaphoreType.DMA((2 + len(f_blocks) + 1,))],
        ),
        out_shape=out_shape,
        compiler_params=pltpu.CompilerParams(vmem_limit_bytes=40 * 1024 * 1024),
        cost_estimate=pl.CostEstimate(
            flops=2 * 2 * LAGS * CH * CH * half * 2 * WIN, bytes_accessed=10 * 2**20, transcendentals=0
        ),
    )(info, tab, *blocks)


def whiten_kernel(bin_dev, info, widths, inverse, low, mid, high, up, down, to_next, to_back, *rest):
    chunks, run = rest[:-1], rest[-1]
    row = info[0]
    half = bin_dev // 2

    def energy(ref, at):
        re, im = ref[0, at].astype(jnp.float32), ref[1, at].astype(jnp.float32)
        return re * re + im * im

    total = jnp.zeros(run.shape[1:], jnp.float32)
    run[0] = total
    for i in range(WMAX):
        total = total + energy(low, i)
        run[i + 1] = total
    for i in range(bin_dev):
        total = total + energy(mid, i)
        run[i + WMAX + 1] = total
    for i in range(WMAX):
        total = total + energy(high, i)
        run[WMAX + bin_dev + i + 1] = total

    def whitened(f):
        w = widths[f]
        mean = (run[f + WMAX + 1 + w] - run[f + WMAX - w]) * inverse[f]
        scale = lax.rsqrt(jnp.maximum(mean, 0.0625))
        return [(mid[part, f].astype(jnp.float32) * scale).astype(jnp.bfloat16) for part in range(2)]

    for f in range(half):
        u = whitened(f)
        d = whitened(f + half)
        for part in range(2):
            up[part, f] = u[part]
            down[part, f] = d[part]
            to_next[part, f] = jnp.where(row < 3, u[part], d[part])
            to_back[part, f] = jnp.where(row > 0, d[part], u[part])
            chunk = sum(f >= start for start in CHUNKS[1:-1])
            chunks[chunk][part, f - CHUNKS[chunk]] = jnp.where(row < 2, u[part], d[part])


def whiten(info, widths, inverse, low, mid, high, rows=16, lanes=256):
    bin_dev = mid.shape[1]
    grid = (WIN // rows, CH // lanes)

    def spec(bins):
        return pl.BlockSpec((2, bins, rows, lanes), lambda w, c, *_: (0, 0, w, c))

    out = jax.ShapeDtypeStruct((2, bin_dev // 2, WIN, CH), jnp.bfloat16)
    sizes = [stop - start for start, stop in zip(CHUNKS, CHUNKS[1:])]
    parts = [jax.ShapeDtypeStruct((2, size, WIN, CH), jnp.bfloat16) for size in sizes]
    return pl.pallas_call(
        functools.partial(whiten_kernel, bin_dev),
        grid_spec=pltpu.PrefetchScalarGridSpec(
            num_scalar_prefetch=3,
            grid=grid,
            in_specs=[spec(WMAX), spec(bin_dev), spec(WMAX)],
            out_specs=[spec(bin_dev // 2)] * 4 + [spec(size) for size in sizes],
            scratch_shapes=[pltpu.VMEM((bin_dev + 2 * WMAX + 1, rows, lanes), jnp.float32)],
        ),
        out_shape=[out] * 4 + parts,
        compiler_params=pltpu.CompilerParams(vmem_limit_bytes=40 * 1024 * 1024),
        cost_estimate=pl.CostEstimate(flops=40 * 2**20, bytes_accessed=15 * 2**20, transcendentals=2**20),
    )(info, widths, inverse, low, mid, high)


def assemble_kernel(flags, places, same_a, same_b, next_a, next_b, back_a, back_b, two_a, two_b, out):
    out[...] = jnp.zeros_like(out)
    rounds = (
        (next_a.at[flags[0]], back_b),
        (two_a.at[flags[2]], two_b),
        (back_a.at[flags[1]], next_b),
        (same_a, same_b),
    )
    for k, (first, second) in enumerate(rounds):
        for i in range(2):
            for j in range(2):
                place = places[(k * 2 + i) * 2 + j]
                columns = pl.ds(j * TILE, TILE)
                for lag in range(LAGS):
                    a = first[lag, i, :, columns].astype(jnp.float32)
                    b = second[lag, i, :, columns].astype(jnp.float32)
                    out[place, lag] = (a + b).astype(jnp.bfloat16)


def assemble(flags, places, *parts):
    return pl.pallas_call(
        assemble_kernel,
        grid_spec=pltpu.PrefetchScalarGridSpec(
            num_scalar_prefetch=2,
            grid=(1,),
            in_specs=[pl.BlockSpec(part.shape, lambda g, *_, n=part.ndim: (0,) * n) for part in parts],
            out_specs=pl.BlockSpec((8 * CAP, LAGS, 32, TILE), lambda g, *_: (0, 0, 0, 0)),
        ),
        out_shape=jax.ShapeDtypeStruct((8 * CAP, LAGS, 32, TILE), jnp.bfloat16),
        compiler_params=pltpu.CompilerParams(vmem_limit_bytes=32 * 1024 * 1024),
    )(flags, places, *parts)


def along_station(value, dx, dy):
    pairs = []
    for x in range(4):
        for y in range(4):
            pairs.append((4 * x + y, 4 * ((x + dx) % 4) + (y + dy) % 4))
    return lax.ppermute(value, "station", pairs)


def along_band(value, target):
    return lax.ppermute(value, "band", [(i, target(i)) for i in range(8)])


def over_bands(partial):
    return lax.psum_scatter(partial, "band", scatter_dimension=0, tiled=False)


def swap_core(value):
    return along_band(value, lambda g: g ^ 1)


def swap_near(value):
    return along_band(value, lambda g: g ^ 2)


def swap_far(value):
    return along_band(value, lambda g: 2 * (3 - g // 2) + g % 2)


def halo(block):
    forward = [(i, i + 1) for i in range(7)]
    backward = [(target, source) for source, target in forward]
    low = lax.ppermute(block[:, block.shape[1] - WMAX :], "band", forward)
    high = lax.ppermute(block[:, :WMAX], "band", backward)
    return low, high


def plus(a, b):
    return a.astype(jnp.float32) + b.astype(jnp.float32)


def pick(value, axis, index):
    return lax.dynamic_index_in_dim(value, index, axis, keepdims=False)


def after(value, token):
    return lax.optimization_barrier((value, token))[0]


def first_sum(mine, got, near, far):
    both = plus(mine, got).astype(jnp.bfloat16).reshape(2, LAGS, 2, 2, 2, 32, mine.shape[-1])
    a, b = both[0], both[1]
    return pick(a, 2, near), pick(b, 3, far), pick(a, 2, 1 - near), pick(b, 3, 1 - far)


def joined(first, second):
    return tuple(jnp.concatenate(pair, axis=-1) for pair in zip(first, second))


def second_sum(keep_a, keep_b, got_a, got_b, near, far):
    a = plus(keep_a, got_a).astype(jnp.bfloat16)
    b = plus(keep_b, got_b).astype(jnp.bfloat16)
    return pick(a, 2, far), pick(b, 2, near), pick(a, 2, 1 - far), pick(b, 2, 1 - near)


def last_sum(keep_a, keep_b, got_a, got_b):
    return plus(keep_a, got_a).astype(jnp.bfloat16), plus(keep_b, got_b).astype(jnp.bfloat16)


def body(spectra, widths, tile_owner):
    bin_dev = spectra.shape[1]
    half = bin_dev // 2
    band = lax.axis_index("band")
    row = lax.axis_index("station") % 4
    depth, core = band // 2, band % 2
    far = depth // 2
    near = (depth % 2) ^ far
    bins_all = bin_dev * 8
    first_bin = band * bin_dev
    normalize = 1.0 / math.sqrt(bins_all * WIN)

    low, high = halo(spectra)
    local_bins = first_bin + jnp.arange(bin_dev)
    count = jnp.minimum(local_bins + widths, bins_all - 1) - jnp.maximum(local_bins - widths, 0) + 1
    inverse = 1.0 / count.astype(jnp.float32)
    row_info = jnp.reshape(row, (1,)).astype(jnp.int32)
    up, down, to_next, to_back, *to_two = whiten(
        row_info, widths, inverse, low, spectra, high
    )
    from_left = along_station(up, 1, 0)
    from_right = along_station(down, -1, 0)
    from_next = along_station(to_next, 0, 1)
    from_back = along_station(to_back, 0, -1)
    from_left, from_right, from_next, from_back = lax.optimization_barrier(
        (from_left, from_right, from_next, from_back)
    )

    lag_index = jnp.arange(1, LAGS).astype(jnp.float32)
    angle = 2.0 * math.pi * (local_bins.astype(jnp.float32)[None, :] * lag_index[:, None]) / bins_all
    cosine, sine = jnp.cos(angle), jnp.sin(angle)
    forth = jnp.stack([cosine, sine])
    back = jnp.stack([cosine, -sine])
    forth_up, forth_down = forth[..., :half], forth[..., half:]
    back_up, back_down = back[..., :half], back[..., half:]

    def info_of(lower):
        return jnp.stack([lower.astype(jnp.int32), core.astype(jnp.int32)])

    def table_of(lower):
        return jnp.where(
            lower, jnp.stack([forth_up, back_up]), jnp.stack([forth_down, back_down])
        )

    def group(blocks, lower, halves):
        others = (up, from_right, from_left, down)
        return edges(info_of(lower), table_of(lower), blocks, others, normalize, halves)

    def two_off(chunk):
        return along_station(chunk, 0, 2)

    def near_swaps(parts):
        return swap_near(parts[2]), swap_far(parts[3])

    def far_swaps(parts):
        return swap_far(parts[2]), swap_near(parts[3])

    chunk0 = two_off(after(to_two[0], (from_next, from_back)))
    same = edges(
        info_of(row >= 0),
        jnp.stack([forth_up, back_down]),
        (from_left,),
        (from_right, up, down),
        normalize,
        False,
    )
    same, chunk0 = lax.optimization_barrier((same, chunk0))
    chunk1 = two_off(after(to_two[1], chunk0))
    same = over_bands(same)
    following, next_send = group((after(from_next, chunk0),), row >= 1, True)
    following, next_send, chunk1 = lax.optimization_barrier((following, next_send, chunk1))
    chunk2 = two_off(after(to_two[2], chunk1))
    next_got = swap_core(next_send)
    behind, back_send = group((after(from_back, following),), row == 3, True)
    following, next_got, behind, back_send, chunk2 = lax.optimization_barrier(
        (following, next_got, behind, back_send, chunk2)
    )
    chunk3 = two_off(after(to_two[3], chunk2))
    back_got = swap_core(back_send)
    following = first_sum(following, next_got, near, far)
    next_got = near_swaps(following)
    behind, back_got, chunk3 = after((behind, back_got, chunk3), following)
    behind = first_sum(behind, back_got, near, far)
    back_got = near_swaps(behind)
    two, two_send = group(after((chunk0, chunk1, chunk2, chunk3), behind), row >= 2, True)
    following, next_got, behind, back_got, two, two_send = lax.optimization_barrier(
        (following, next_got, behind, back_got, two, two_send)
    )
    two_got = swap_core(two_send)
    following = second_sum(*following[:2], *next_got, near, far)
    next_got = far_swaps(following)
    behind = second_sum(*after(behind[:2], following), *back_got, near, far)
    back_got = far_swaps(behind)
    two, two_got = after((two, two_got), behind)
    two = first_sum(two, two_got, near, far)
    two_got = near_swaps(two)
    next_a, next_b = last_sum(*after(following[:2], behind), *next_got)
    same_a, same_b = same[0], same[1]
    right = along_station(jnp.stack([same_b, next_a]), 1, 0)
    back_a, back_b = last_sum(*after(behind[:2], (two, next_a)), *back_got)
    back_right = along_station(back_a, 1, 0)
    back_b = along_station(back_b, 0, 1)
    two, right = after((two, right), back_a)
    two = second_sum(*two[:2], *two_got, near, far)
    two, right = lax.optimization_barrier((two, right))
    two_got = far_swaps(two)
    next_b = along_station(after(next_b, two), 0, -1)
    back_right, back_b = after((back_right, back_b), two)
    two_a, two_b = last_sum(*after(two[:2], (back_right, back_b)), *two_got)
    two_right = along_station(two_a, 1, 0)
    two_b = along_station(two_b, 0, 2)
    flags = jnp.stack([row < 1, row != 3, row < 2]).astype(jnp.int32)
    parts = (
        same_a,
        right[0],
        jnp.stack([next_a, right[1]]),
        next_b,
        jnp.stack([back_a, back_right]),
        back_b,
        jnp.stack([two_a, two_right]),
        two_b,
    )

    tiles_block = tile_owner.shape[0]
    owners = tile_owner[:, 0]
    order = jnp.arange(tiles_block)
    earlier = (order[:, None] > order[None, :]) & (owners[:, None] == owners[None, :])
    slot_index = jnp.sum(jnp.where(earlier, 1, 0), axis=1).astype(jnp.int32)
    buffer = assemble(flags, owners * CAP + slot_index, *parts).reshape(8, CAP, LAGS, 32, TILE)
    arrived = lax.all_to_all(buffer, "band", split_axis=0, concat_axis=0, tiled=True)
    pieces = [arrived[g] for _, g in sorted((r, g) for g, r in enumerate(ROWS_OF))]
    result = jnp.stack(pieces, axis=2).astype(jnp.float32)
    return result.reshape(1, 1, CAP, LAGS, TILE, TILE)


def solution(mesh):
    return jax.shard_map(
        body,
        mesh=mesh,
        in_specs=(P(None, "band", None, "station"), P("band"), P("station", None)),
        out_specs=P("station", "band", None, None, None, None),
        check_vma=False,
    )
```

```python
import functools
import math

import jax
import jax.numpy as jnp
from jax import lax
from jax.experimental import pallas as pl
from jax.experimental.pallas import tpu as pltpu
from jax.sharding import PartitionSpec as P

TILE = 256
TDEV = 2
LAGS = 3
ROUNDS = 4
WMAX = 8
CAP = 4
CH = TILE * TDEV
WIN = 32
CHUNKS = (0, 9, 19, 28, 32)
ROWS_OF = (0, 4, 2, 6, 3, 7, 1, 5)


def edge_kernel(normalize, choose, half, starts, halves, info, tab, *refs):
    pieces = len(starts)
    f_hbm, refs = refs[:pieces], refs[pieces:]
    if choose:
        t_up, t_down, q_up, q_down, *outs, f_buf, t_buf, q_buf, ft, tt, qt, sems = refs
    else:
        fb_hbm, t_hbm, q_hbm, *outs, f_buf, fb_buf, t_buf, q_buf, ft, ftb, tt, qt, sems = refs
    lag = pl.program_id(0)
    core = info[1]
    rows = 2 * half * WIN

    def turn(buf, out, which, k):
        for b in range(half):
            span = pl.ds(b * WIN, WIN)
            re, im = buf[0, b].astype(jnp.float32), buf[1, b].astype(jnp.float32)
            c, s = tab[which, 0, k, b], tab[which, 1, k, b]
            out[0, span] = (re * c + im * s).astype(jnp.bfloat16)
            out[1, span] = (im * c - re * s).astype(jnp.bfloat16)

    def transpose(buf, out):
        flat = buf[...].reshape(rows, CH)
        for h in range(rows // 512):
            out[:, h * 512 : (h + 1) * 512] = flat[h * 512 : (h + 1) * 512].T

    def store(e, p):
        p = (p * normalize).astype(jnp.bfloat16)
        for i in range(2):
            tile = p[i * TILE : (i + 1) * TILE]
            if halves:
                lo, hi = tile[: TILE // 2], tile[TILE // 2 :]
                outs[0][e, 0, i] = jnp.where(core == 0, lo, hi)
                outs[1][e, 0, i] = jnp.where(core == 0, hi, lo)
            else:
                for g in range(8):
                    outs[0][g, e, 0, i] = tile[ROWS_OF[g] * 32 : (ROWS_OF[g] + 1) * 32]

    def product_a(t):
        store(0, jnp.dot(ft[...], t.reshape(rows, CH), preferred_element_type=jnp.float32).T)

    def product_b(q):
        flip = ft if choose else ftb
        store(1, jnp.dot(flip[...], q.reshape(rows, CH), preferred_element_type=jnp.float32))

    @pl.when(lag == 0)
    def _():
        if choose:
            loads = [
                pltpu.make_async_copy(src, f_buf.at[:, pl.ds(starts[n], src.shape[1])], sems.at[2 + n])
                for n, src in enumerate(f_hbm)
            ]
            for load in loads:
                load.start()
            lower = info[0] > 0

            @pl.when(lower)
            def _():
                pltpu.make_async_copy(t_up, t_buf, sems.at[0]).start()
                pltpu.make_async_copy(q_up, q_buf, sems.at[1]).start()

            @pl.when(jnp.logical_not(lower))
            def _():
                pltpu.make_async_copy(t_down, t_buf, sems.at[0]).start()
                pltpu.make_async_copy(q_down, q_buf, sems.at[1]).start()

            for load in loads:
                load.wait()
            transpose(f_buf, ft)
            pltpu.make_async_copy(t_up, t_buf, sems.at[0]).wait()
            pltpu.make_async_copy(q_up, q_buf, sems.at[1]).wait()
        else:
            copies = [
                pltpu.make_async_copy(src, dst, sems.at[n])
                for n, (src, dst) in enumerate(
                    ((f_hbm[0], f_buf), (fb_hbm, fb_buf), (t_hbm, t_buf), (q_hbm, q_buf))
                )
            ]
            for copy in copies:
                copy.start()
            copies[0].wait()
            transpose(f_buf, ft)
            copies[1].wait()
            transpose(fb_buf, ftb)
            copies[2].wait()
            copies[3].wait()
        turn(t_buf, tt, 0, 0)
        turn(q_buf, qt, 1, 0)
        product_a(t_buf[...])
        product_b(q_buf[...])

    @pl.when(lag == 1)
    def _():
        product_a(tt[...])
        product_b(qt[...])

    @pl.when(lag == 2)
    def _():
        turn(t_buf, tt, 0, 1)
        turn(q_buf, qt, 1, 1)
        product_a(tt[...])
        product_b(qt[...])


def edges(info, tab, f_blocks, others, normalize, halves):
    half = others[0].shape[1]
    choose = len(others) == 4
    starts = [sum(block.shape[1] for block in f_blocks[:n]) for n in range(len(f_blocks))]
    if halves:
        shape, part = (2, LAGS, 2, TILE // 2, CH), (2, 1, 2, TILE // 2, CH)
        out_spec = [pl.BlockSpec(part, lambda l, info, tab: (0, l, 0, 0, 0))] * 2
        out_shape = [jax.ShapeDtypeStruct(shape, jnp.bfloat16)] * 2
    else:
        shape, part = (8, 2, LAGS, 2, 32, CH), (8, 2, 1, 2, 32, CH)
        out_spec = pl.BlockSpec(part, lambda l, info, tab: (0, 0, l, 0, 0, 0))
        out_shape = jax.ShapeDtypeStruct(shape, jnp.bfloat16)
    buf = pltpu.VMEM((2, half, WIN, CH), jnp.bfloat16)
    flipped = pltpu.VMEM((CH, 2 * half * WIN), jnp.bfloat16)
    turned = pltpu.VMEM((2, half * WIN, CH), jnp.bfloat16)
    if choose:
        scratch = [buf] * 3 + [flipped] + [turned] * 2
    else:
        scratch = [buf] * 4 + [flipped] * 2 + [turned] * 2
    blocks = (*f_blocks, *others)
    return pl.pallas_call(
        functools.partial(edge_kernel, normalize, choose, half, starts, halves),
        grid_spec=pltpu.PrefetchScalarGridSpec(
            num_scalar_prefetch=2,
            grid=(LAGS,),
            in_specs=[pl.BlockSpec(memory_space=pl.ANY)] * len(blocks),
            out_specs=out_spec,
            scratch_shapes=scratch + [pltpu.SemaphoreType.DMA((2 + len(f_blocks) + 1,))],
        ),
        out_shape=out_shape,
        compiler_params=pltpu.CompilerParams(vmem_limit_bytes=40 * 1024 * 1024),
        cost_estimate=pl.CostEstimate(
            flops=2 * 2 * LAGS * CH * CH * half * 2 * WIN, bytes_accessed=10 * 2**20, transcendentals=0
        ),
    )(info, tab, *blocks)


def whiten_kernel(bin_dev, info, widths, inverse, low, mid, high, up, down, to_next, to_back, *rest):
    chunks, run = rest[:-1], rest[-1]
    row = info[0]
    half = bin_dev // 2

    def energy(ref, at):
        re, im = ref[0, at].astype(jnp.float32), ref[1, at].astype(jnp.float32)
        return re * re + im * im

    total = jnp.zeros(run.shape[1:], jnp.float32)
    run[0] = total
    for i in range(WMAX):
        total = total + energy(low, i)
        run[i + 1] = total
    for i in range(bin_dev):
        total = total + energy(mid, i)
        run[i + WMAX + 1] = total
    for i in range(WMAX):
        total = total + energy(high, i)
        run[WMAX + bin_dev + i + 1] = total

    def whitened(f):
        w = widths[f]
        mean = (run[f + WMAX + 1 + w] - run[f + WMAX - w]) * inverse[f]
        scale = lax.rsqrt(jnp.maximum(mean, 0.0625))
        return [(mid[part, f].astype(jnp.float32) * scale).astype(jnp.bfloat16) for part in range(2)]

    for f in range(half):
        u = whitened(f)
        d = whitened(f + half)
        for part in range(2):
            up[part, f] = u[part]
            down[part, f] = d[part]
            to_next[part, f] = jnp.where(row < 3, u[part], d[part])
            to_back[part, f] = jnp.where(row > 0, d[part], u[part])
            chunk = sum(f >= start for start in CHUNKS[1:-1])
            chunks[chunk][part, f - CHUNKS[chunk]] = jnp.where(row < 2, u[part], d[part])


def whiten(info, widths, inverse, low, mid, high, rows=16, lanes=256):
    bin_dev = mid.shape[1]
    grid = (WIN // rows, CH // lanes)

    def spec(bins):
        return pl.BlockSpec((2, bins, rows, lanes), lambda w, c, *_: (0, 0, w, c))

    out = jax.ShapeDtypeStruct((2, bin_dev // 2, WIN, CH), jnp.bfloat16)
    sizes = [stop - start for start, stop in zip(CHUNKS, CHUNKS[1:])]
    parts = [jax.ShapeDtypeStruct((2, size, WIN, CH), jnp.bfloat16) for size in sizes]
    return pl.pallas_call(
        functools.partial(whiten_kernel, bin_dev),
        grid_spec=pltpu.PrefetchScalarGridSpec(
            num_scalar_prefetch=3,
            grid=grid,
            in_specs=[spec(WMAX), spec(bin_dev), spec(WMAX)],
            out_specs=[spec(bin_dev // 2)] * 4 + [spec(size) for size in sizes],
            scratch_shapes=[pltpu.VMEM((bin_dev + 2 * WMAX + 1, rows, lanes), jnp.float32)],
        ),
        out_shape=[out] * 4 + parts,
        compiler_params=pltpu.CompilerParams(vmem_limit_bytes=40 * 1024 * 1024),
        cost_estimate=pl.CostEstimate(flops=40 * 2**20, bytes_accessed=15 * 2**20, transcendentals=2**20),
    )(info, widths, inverse, low, mid, high)


def assemble_kernel(flags, places, same_a, same_b, next_a, next_b, back_a, back_b, two_a, two_b, out):
    out[...] = jnp.zeros_like(out)
    rounds = (
        (next_a.at[flags[0]], back_b),
        (two_a.at[flags[2]], two_b),
        (back_a.at[flags[1]], next_b),
        (same_a, same_b),
    )
    for k, (first, second) in enumerate(rounds):
        for i in range(2):
            for j in range(2):
                place = places[(k * 2 + i) * 2 + j]
                columns = pl.ds(j * TILE, TILE)
                for lag in range(LAGS):
                    a = first[lag, i, :, columns].astype(jnp.float32)
                    b = second[lag, i, :, columns].astype(jnp.float32)
                    out[place, lag] = (a + b).astype(jnp.bfloat16)


def assemble(flags, places, *parts):
    return pl.pallas_call(
        assemble_kernel,
        grid_spec=pltpu.PrefetchScalarGridSpec(
            num_scalar_prefetch=2,
            grid=(1,),
            in_specs=[pl.BlockSpec(part.shape, lambda g, *_, n=part.ndim: (0,) * n) for part in parts],
            out_specs=pl.BlockSpec((8 * CAP, LAGS, 32, TILE), lambda g, *_: (0, 0, 0, 0)),
        ),
        out_shape=jax.ShapeDtypeStruct((8 * CAP, LAGS, 32, TILE), jnp.bfloat16),
        compiler_params=pltpu.CompilerParams(vmem_limit_bytes=32 * 1024 * 1024),
    )(flags, places, *parts)


def along_station(value, dx, dy):
    pairs = []
    for x in range(4):
        for y in range(4):
            pairs.append((4 * x + y, 4 * ((x + dx) % 4) + (y + dy) % 4))
    return lax.ppermute(value, "station", pairs)


def along_band(value, target):
    return lax.ppermute(value, "band", [(i, target(i)) for i in range(8)])


def over_bands(partial):
    return lax.psum_scatter(partial, "band", scatter_dimension=0, tiled=False)


def swap_core(value):
    return along_band(value, lambda g: g ^ 1)


def swap_near(value):
    return along_band(value, lambda g: g ^ 2)


def swap_far(value):
    return along_band(value, lambda g: 2 * (3 - g // 2) + g % 2)


def halo(block):
    forward = [(i, i + 1) for i in range(7)]
    backward = [(target, source) for source, target in forward]
    low = lax.ppermute(block[:, block.shape[1] - WMAX :], "band", forward)
    high = lax.ppermute(block[:, :WMAX], "band", backward)
    return low, high


def plus(a, b):
    return a.astype(jnp.float32) + b.astype(jnp.float32)


def pick(value, axis, index):
    return lax.dynamic_index_in_dim(value, index, axis, keepdims=False)


def after(value, token):
    return lax.optimization_barrier((value, token))[0]


def first_sum(mine, got, near, far):
    both = plus(mine, got).astype(jnp.bfloat16).reshape(2, LAGS, 2, 2, 2, 32, mine.shape[-1])
    a, b = both[0], both[1]
    return pick(a, 2, near), pick(b, 3, far), pick(a, 2, 1 - near), pick(b, 3, 1 - far)


def joined(first, second):
    return tuple(jnp.concatenate(pair, axis=-1) for pair in zip(first, second))


def second_sum(keep_a, keep_b, got_a, got_b, near, far):
    a = plus(keep_a, got_a).astype(jnp.bfloat16)
    b = plus(keep_b, got_b).astype(jnp.bfloat16)
    return pick(a, 2, far), pick(b, 2, near), pick(a, 2, 1 - far), pick(b, 2, 1 - near)


def last_sum(keep_a, keep_b, got_a, got_b):
    return plus(keep_a, got_a).astype(jnp.bfloat16), plus(keep_b, got_b).astype(jnp.bfloat16)


def body(spectra, widths, tile_owner):
    bin_dev = spectra.shape[1]
    half = bin_dev // 2
    band = lax.axis_index("band")
    row = lax.axis_index("station") % 4
    depth, core = band // 2, band % 2
    far = depth // 2
    near = (depth % 2) ^ far
    bins_all = bin_dev * 8
    first_bin = band * bin_dev
    normalize = 1.0 / math.sqrt(bins_all * WIN)

    low, high = halo(spectra)
    local_bins = first_bin + jnp.arange(bin_dev)
    count = jnp.minimum(local_bins + widths, bins_all - 1) - jnp.maximum(local_bins - widths, 0) + 1
    inverse = 1.0 / count.astype(jnp.float32)
    row_info = jnp.reshape(row, (1,)).astype(jnp.int32)
    up, down, to_next, to_back, *to_two = whiten(
        row_info, widths, inverse, low, spectra, high
    )
    from_left = along_station(up, 1, 0)
    from_right = along_station(down, -1, 0)
    from_next = along_station(to_next, 0, 1)
    from_back = along_station(to_back, 0, -1)
    from_left, from_right, from_next, from_back = lax.optimization_barrier(
        (from_left, from_right, from_next, from_back)
    )

    lag_index = jnp.arange(1, LAGS).astype(jnp.float32)
    angle = 2.0 * math.pi * (local_bins.astype(jnp.float32)[None, :] * lag_index[:, None]) / bins_all
    cosine, sine = jnp.cos(angle), jnp.sin(angle)
    forth = jnp.stack([cosine, sine])
    back = jnp.stack([cosine, -sine])
    forth_up, forth_down = forth[..., :half], forth[..., half:]
    back_up, back_down = back[..., :half], back[..., half:]

    def info_of(lower):
        return jnp.stack([lower.astype(jnp.int32), core.astype(jnp.int32)])

    def table_of(lower):
        return jnp.where(
            lower, jnp.stack([forth_up, back_up]), jnp.stack([forth_down, back_down])
        )

    def group(blocks, lower, halves):
        others = (up, from_right, from_left, down)
        return edges(info_of(lower), table_of(lower), blocks, others, normalize, halves)

    def two_off(chunk):
        return along_station(chunk, 0, 2)

    def near_swaps(parts):
        return swap_near(parts[2]), swap_far(parts[3])

    def far_swaps(parts):
        return swap_far(parts[2]), swap_near(parts[3])

    chunk0 = two_off(after(to_two[0], (from_next, from_back)))
    same = edges(
        info_of(row >= 0),
        jnp.stack([forth_up, back_down]),
        (from_left,),
        (from_right, up, down),
        normalize,
        False,
    )
    same, chunk0 = lax.optimization_barrier((same, chunk0))
    chunk1 = two_off(after(to_two[1], chunk0))
    same = over_bands(same)
    following, next_send = group((after(from_next, chunk0),), row >= 1, True)
    following, next_send, chunk1 = lax.optimization_barrier((following, next_send, chunk1))
    chunk2 = two_off(after(to_two[2], chunk1))
    next_got = swap_core(next_send)
    behind, back_send = group((after(from_back, following),), row == 3, True)
    following, next_got, behind, back_send, chunk2 = lax.optimization_barrier(
        (following, next_got, behind, back_send, chunk2)
    )
    chunk3 = two_off(after(to_two[3], chunk2))
    back_got = swap_core(back_send)
    following = first_sum(following, next_got, near, far)
    next_got = near_swaps(following)
    behind, back_got, chunk3 = after((behind, back_got, chunk3), following)
    behind = first_sum(behind, back_got, near, far)
    back_got = near_swaps(behind)
    two, two_send = group(after((chunk0, chunk1, chunk2, chunk3), behind), row >= 2, True)
    following, next_got, behind, two, two_send = lax.optimization_barrier(
        (following, next_got, behind, two, two_send)
    )
    two_got = swap_core(two_send)
    following = second_sum(*following[:2], *next_got, near, far)
    next_got = far_swaps(following)
    behind = second_sum(*after(behind[:2], following), *back_got, near, far)
    back_got = far_swaps(behind)
    two, two_got = after((two, two_got), behind)
    two = first_sum(two, two_got, near, far)
    two_got = near_swaps(two)
    next_a, next_b = last_sum(*after(following[:2], behind), *next_got)
    same_a, same_b = same[0], same[1]
    right = along_station(jnp.stack([same_b, next_a]), 1, 0)
    back_a, back_b = last_sum(*after(behind[:2], (two, next_a)), *back_got)
    back_right = along_station(back_a, 1, 0)
    back_b = along_station(back_b, 0, 1)
    two, right = after((two, right), back_a)
    two = second_sum(*two[:2], *two_got, near, far)
    two, right = lax.optimization_barrier((two, right))
    two_got = far_swaps(two)
    next_b = along_station(after(next_b, two), 0, -1)
    back_right, back_b = after((back_right, back_b), two)
    two_a, two_b = last_sum(*after(two[:2], (back_right, back_b)), *two_got)
    two_right = along_station(two_a, 1, 0)
    two_b = along_station(two_b, 0, 2)
    flags = jnp.stack([row < 1, row != 3, row < 2]).astype(jnp.int32)
    parts = (
        same_a,
        right[0],
        jnp.stack([next_a, right[1]]),
        next_b,
        jnp.stack([back_a, back_right]),
        back_b,
        jnp.stack([two_a, two_right]),
        two_b,
    )

    tiles_block = tile_owner.shape[0]
    owners = tile_owner[:, 0]
    order = jnp.arange(tiles_block)
    earlier = (order[:, None] > order[None, :]) & (owners[:, None] == owners[None, :])
    slot_index = jnp.sum(jnp.where(earlier, 1, 0), axis=1).astype(jnp.int32)
    buffer = assemble(flags, owners * CAP + slot_index, *parts).reshape(8, CAP, LAGS, 32, TILE)
    arrived = lax.all_to_all(buffer, "band", split_axis=0, concat_axis=0, tiled=True)
    pieces = [arrived[g] for _, g in sorted((r, g) for g, r in enumerate(ROWS_OF))]
    result = jnp.stack(pieces, axis=2).astype(jnp.float32)
    return result.reshape(1, 1, CAP, LAGS, TILE, TILE)


def solution(mesh):
    return jax.shard_map(
        body,
        mesh=mesh,
        in_specs=(P(None, "band", None, "station"), P("band"), P("station", None)),
        out_specs=P("station", "band", None, None, None, None),
        check_vma=False,
    )
```
